32 devices in a mesh: prow: 8 (over z, core), pcol: 4 (over y, x).
Axes of the slice: x: 2, y: 2, z: 4, core: 2. Of those that a mesh axis runs over, the one named last changes fastest.
Arguments:
- root_inverse: float32 [4, 8, 128, 8, 4, 128], P(None, 'prow', None, None, 'pcol'), as said below
- lower_one: float32 [4, 8, 128, 4, 4, 128], P(None, 'prow', None, None, 'pcol'), may hold values from -0.125 to 0.125
- lower_two: float32 [6, 8, 128, 4, 4, 128], P(None, 'prow', None, None, 'pcol'), may hold values from -0.15625 to 0.15625
- dinv_one: float32 [2, 8, 128, 4, 4, 128], P(None, 'prow', None, None, 'pcol'), as said below
- dinv_two: float32 [2, 8, 128, 4, 4, 128], P(None, 'prow', None, None, 'pcol'), as said below
- seg_one: int32 [16], replicated, may hold values from 0 to 2, as said below
- seg_two: int32 [16], replicated, may hold values from 0 to 3, as said below
- parent_two: int32 [4], replicated, may hold values from 0 to 2
- pattern_one: int32 [3, 32], replicated, may hold values 0 or 1
- pattern_two: int32 [4, 48], replicated, may hold values 0 or 1
Outputs:
- inverse_one: float32 [2, 8, 128, 4, 4, 128], P(None, 'prow', None, None, 'pcol')
- inverse_two: float32 [2, 8, 128, 4, 4, 128], P(None, 'prow', None, None, 'pcol')
The draws below stay inside these ranges and needn't reach their ends.
Inputs may be any that keep to these rules, and one draw needn't show every extreme that they name: `root_inverse`: Block-diagonal over supernodes is not implied; this is a symmetric matrix. `dinv_one`: Symmetric, and zero in every block whose row and column blocks belong to different supernodes of seg_one. `dinv_two`: Symmetric, and zero in every block whose row and column blocks belong to different supernodes of seg_two. `seg_one`: never falls; every supernode 0 to 2 has 1 to 8 consecutive blocks, one exactly 8. `seg_two`: never falls; every supernode 0 to 3 has 1 to 8 consecutive blocks, one exactly 8.
All inputs are finite; a program needn't handle non-finite values.
Results may differ from the reference program's by a relative error of at most 0.00005.
Values sent between devices are 32-bit elements; how exact they have to be, the bound alone decides.
No kernel may reach another device: no remote copies, remote signals or barrier semaphores. Data moves between devices by JAX's collectives and lax.ppermute only.
A program may use at most 128 MiB of HBM per device.

```python
import math
import jax
import jax.numpy as jnp
from jax import lax

B = 128
NR = 32
W1 = 16
W2 = 16
C1 = 3
C2 = 4
R2 = 48
N_PROW = 8
N_PCOL = 4


def segment_ids(key, block_total, supernodes):
    biggest = block_total // 2
    remainder = block_total - biggest
    where_big = jax.random.randint(jax.random.fold_in(key, 1), (), 0, supernodes)
    shuffled = jax.random.permutation(jax.random.fold_in(key, 2), remainder - 1) + 1
    cut_points = jnp.sort(shuffled[:supernodes - 2]).astype(jnp.int32)
    bounds = jnp.concatenate([jnp.zeros((1,), jnp.int32), cut_points, jnp.full((1,), remainder, jnp.int32)])
    smaller = bounds[1:] - bounds[:-1]
    padded = jnp.concatenate([smaller, jnp.zeros((1,), jnp.int32)])
    shifted = jnp.concatenate([jnp.zeros((1,), jnp.int32), smaller])
    position = jnp.arange(supernodes, dtype=jnp.int32)
    sizes_all = jnp.where(position < where_big, padded, jnp.where(position == where_big, biggest, shifted))
    endings = jnp.cumsum(sizes_all)
    block_ids = jnp.arange(block_total, dtype=jnp.int32)
    return jnp.sum((block_ids[:, None] >= endings[None, :]).astype(jnp.int32), axis=1).astype(jnp.int32)


def symmetric_body(key, order, spread):
    raw_values = jax.random.normal(jax.random.fold_in(key, 3), (order, order), jnp.float32)
    diagonal = 1.0 + jax.random.uniform(jax.random.fold_in(key, 4), (order,), jnp.float32, 0.0, 1.0)
    off_part = (raw_values + raw_values.T) * 0.5 * spread
    return off_part + jnp.diag(diagonal)


def supernode_inverse(key, block_total, seg_ids):
    order = block_total * B
    matrix = symmetric_body(key, order, 0.6 / math.sqrt(block_total // 2 * B))
    member = seg_ids[jnp.arange(order, dtype=jnp.int32) // B]
    same_node = member[:, None] == member[None, :]
    kept = jnp.where(same_node, matrix, 0.0).astype(jnp.float32)
    return kept.reshape(block_total // N_PROW, N_PROW, B, block_total // N_PCOL, N_PCOL, B)


def draw_root_inverse(key, part):
    order = NR * B
    matrix = symmetric_body(jax.random.fold_in(key, 31), order, 0.6 / math.sqrt(order))
    return matrix.astype(jnp.float32).reshape(NR // N_PROW, N_PROW, B, NR // N_PCOL, N_PCOL, B)


def draw_seg_one(key, part):
    return segment_ids(jax.random.fold_in(key, 11), W1, C1)


def draw_dinv_one(key, part):
    seg_ids = segment_ids(jax.random.fold_in(key, 11), W1, C1)
    return supernode_inverse(jax.random.fold_in(key, 12), W1, seg_ids)


def draw_seg_two(key, part):
    return segment_ids(jax.random.fold_in(key, 21), W2, C2)


def draw_dinv_two(key, part):
    seg_ids = segment_ids(jax.random.fold_in(key, 21), W2, C2)
    return supernode_inverse(jax.random.fold_in(key, 22), W2, seg_ids)


def with_ends(drawn, key, smallest, high):
    index_at = [jax.random.randint(jax.random.fold_in(key, axis), (), 0, length) for axis, length in enumerate(drawn.shape)]
    longest = drawn.shape.index(max(drawn.shape))
    neighbour = index_at[:longest] + [(index_at[longest] + 1) % drawn.shape[longest]] + index_at[longest + 1:]
    return drawn.at[tuple(index_at)].set(smallest).at[tuple(neighbour)].set(high)


def level_of(own_key, extent, shards, low, high):
    factor_of, own = 1.0, jax.random.fold_in(own_key, 6)
    for axis_at, shards_of in shards:
        steps = jnp.exp(jax.random.uniform(jax.random.fold_in(own, axis_at), (shards_of,), jnp.float32, low / len(shards), high / len(shards)))
        factor_of = factor_of * jnp.repeat(steps, extent[axis_at] // shards_of).reshape([-1 if axis == axis_at else 1 for axis in range(len(extent))])
    return factor_of


def gaussian(key, shape, deviation, bound, cuts=(), kind=jnp.bfloat16):
    factor_of = level_of(key, shape, cuts, -0.22, 0.18) if cuts else 1.0
    entries = jax.random.normal(key, shape, jnp.float32) * deviation * factor_of
    return jnp.minimum(jnp.maximum(entries, -bound), bound).astype(kind)


def setup_inputs(seed: int = 0) -> dict:
    splits = jax.random.split(jax.random.key(seed), 11)
    return {
        "root_inverse": draw_root_inverse(jax.random.fold_in(splits[10], 71), 0),
        "lower_one": gaussian(splits[1], (NR // N_PROW, N_PROW, B, W1 // N_PCOL, N_PCOL, B), (NR * B // 2) ** -0.5, 0.125, ((1, 8), (4, 4)), jnp.float32),
        "lower_two": gaussian(splits[2], (R2 // N_PROW, N_PROW, B, W2 // N_PCOL, N_PCOL, B), (R2 * B // 4) ** -0.5, 0.15625, ((1, 8), (4, 4)), jnp.float32),
        "dinv_one": draw_dinv_one(jax.random.fold_in(splits[10], 71), 0),
        "dinv_two": draw_dinv_two(jax.random.fold_in(splits[10], 71), 0),
        "seg_one": draw_seg_one(jax.random.fold_in(splits[10], 71), 0),
        "seg_two": draw_seg_two(jax.random.fold_in(splits[10], 71), 0),
        "parent_two": with_ends(jax.random.randint(splits[7], (C2,), 0, C1), jax.random.fold_in(splits[7], 1), 0, C1 - 1).astype(jnp.int32),
        "pattern_one": with_ends((jax.random.randint(splits[8], (C1, NR), 0, 2) < 1).astype(jnp.int32), jax.random.fold_in(splits[8], 1), 0, 1),
        "pattern_two": with_ends((jax.random.randint(splits[9], (C2, R2), 0, 2) < 1).astype(jnp.int32), jax.random.fold_in(splits[9], 1), 0, 1),
    }


def as_matrix(blocks):
    shape_now = blocks.shape
    return blocks.reshape(shape_now[0] * shape_now[1] * shape_now[2], shape_now[3] * shape_now[4] * shape_now[5])


def as_blocks(matrix, block_rows, block_cols):
    return matrix.reshape(block_rows // N_PROW, N_PROW, B, block_cols // N_PCOL, N_PCOL, B)


def expand(block_mask):
    return jnp.repeat(jnp.repeat(block_mask, B, axis=0), B, axis=1)


def product(left_side, right_side):
    return jnp.dot(left_side, right_side, precision=lax.Precision.HIGHEST, preferred_element_type=jnp.float32)


def reference(root_inverse, lower_one, lower_two, dinv_one, dinv_two, seg_one, seg_two, parent_two, pattern_one, pattern_two):
    root_matrix = as_matrix(root_inverse)
    mask_one = pattern_one[seg_one, :].T.astype(jnp.float32)
    masked_one = as_matrix(lower_one) * expand(mask_one)
    solved_one = product(root_matrix, masked_one)
    same_one = (seg_one[:, None] == seg_one[None, :]).astype(jnp.float32)
    inverse_one = (as_matrix(dinv_one) + product(masked_one.T, solved_one)) * expand(same_one)
    region = jnp.concatenate([
        jnp.concatenate([root_matrix, -solved_one], axis=1),
        jnp.concatenate([-solved_one.T, inverse_one], axis=1)], axis=0)
    parent_of = parent_two[seg_two]
    root_reach = pattern_one[parent_of, :]
    level_reach = (seg_one[None, :] == parent_of[:, None]).astype(jnp.int32)
    reachable = jnp.concatenate([root_reach, level_reach], axis=1)
    mask_two = (pattern_two[seg_two, :] * reachable).T.astype(jnp.float32)
    masked_two = as_matrix(lower_two) * expand(mask_two)
    solved_two = product(region, masked_two)
    same_two = (seg_two[:, None] == seg_two[None, :]).astype(jnp.float32)
    inverse_two = (as_matrix(dinv_two) + product(masked_two.T, solved_two)) * expand(same_two)
    return as_blocks(inverse_one, W1, W1), as_blocks(inverse_two, W2, W2)
```

```python
import functools

import jax
import jax.numpy as jnp
from jax import lax
from jax.experimental import pallas as pl
from jax.experimental.pallas import tpu as pltpu
from jax.sharding import PartitionSpec as P

VMEM_LIMIT = 56 * 1024 * 1024
F32 = jnp.float32
BOTH = ("prow", "pcol")


def halves(value):
    high = value.astype(jnp.bfloat16)
    low = (value - high.astype(F32)).astype(jnp.bfloat16)
    return high, low


def product(left, right):
    left_high, left_low = left
    right_high, right_low = right
    dot = functools.partial(jnp.dot, preferred_element_type=F32)
    return dot(left_high, right_high) + (dot(left_high, right_low) + dot(left_low, right_high))


def vmem_call(kernel, outs, smem_args, vmem_args, scratch=(), flops=0, after=()):
    def body(*refs):
        kernel(*refs[len(after) :])

    return pl.pallas_call(
        body,
        out_shape=outs,
        in_specs=[pl.BlockSpec(memory_space=pl.ANY)] * len(after)
        + [pl.BlockSpec(memory_space=pltpu.SMEM)] * len(smem_args)
        + [pl.BlockSpec(memory_space=pltpu.VMEM)] * len(vmem_args),
        out_specs=jax.tree.map(lambda _: pl.BlockSpec(memory_space=pltpu.VMEM), outs),
        scratch_shapes=scratch,
        compiler_params=pltpu.CompilerParams(vmem_limit_bytes=VMEM_LIMIT),
        cost_estimate=pl.CostEstimate(
            flops=flops,
            bytes_accessed=sum(4 * arg.size for arg in vmem_args),
            transcendentals=0,
        ),
    )(*after, *smem_args, *vmem_args)


def out_shape(*dims):
    return jax.ShapeDtypeStruct(dims, F32)


class Layout:
    def __init__(self, prow, pcol, width):
        self.prow, self.pcol, self.width = prow, pcol, width
        self.ratio = prow // pcol

    def blocks(self, columns):
        for part in range(self.ratio):
            for group in range(columns // self.ratio):
                yield part * (columns // self.ratio) + group, group * self.ratio + part

    def column_id(self, column, pcol_place):
        return column * self.pcol + pcol_place

    def read(self, ref, row, column, columns):
        return ref[pl.ds(row * self.width * columns + column, self.width, stride=columns), :]

    def lanes(self, index):
        return slice(index * self.width, (index + 1) * self.width)


def first_kernel(lay, counts, place_ref, seg_one, seg_two, parent, one, two, lower_one, lower_two, *outs):
    first_ref, level_ref = outs
    root_count, level_count, one_columns, two_columns, root_total = counts
    prow_place, pcol_place = place_ref[0], place_ref[1]
    for index, column in lay.blocks(one_columns):
        node = seg_one[lay.column_id(column, pcol_place)]
        for row in range(root_count):
            keep = one[node, row * lay.prow + prow_place]
            block = lay.read(lower_one, row, column, one_columns)
            first_ref[lay.lanes(row), lay.lanes(index)] = block * keep.astype(F32)
    for index, column in lay.blocks(two_columns):
        node = seg_two[lay.column_id(column, pcol_place)]
        above = parent[node]
        total = jnp.zeros((lay.width, lay.width), F32)
        for row in range(level_count):
            level_row = row * lay.prow + prow_place
            keep = jnp.where(seg_one[level_row] == above, two[node, root_total + level_row], 0)
            block = lay.read(lower_two, root_count + row, column, two_columns)
            total = total + block * keep.astype(F32)
        level_ref[:, lay.lanes(index)] = total


def root_kernel(lay, root_count, root_columns, root, root_ref):
    for index, column in lay.blocks(root_columns):
        for row in range(root_count):
            block = lay.read(root, row, column, root_columns)
            root_ref[lay.lanes(row), lay.lanes(index)] = block


def second_kernel(lay, counts, place_ref, seg_two, parent, one, two, lower_two, dinv, *refs):
    level_refs = refs[:-3]
    second_ref, dinv_ref, stack_ref = refs[-3:]
    for slot, level_ref in enumerate(level_refs):
        stack_ref[slot] = level_ref[...]
    root_count, level_count, one_columns, two_columns, root_total = counts
    prow_place, pcol_place = place_ref[0], place_ref[1]
    for index, column in lay.blocks(two_columns):
        node = seg_two[lay.column_id(column, pcol_place)]
        above = parent[node]
        for row in range(root_count):
            root_row = row * lay.prow + prow_place
            keep = two[node, root_row] * one[above, root_row]
            block = lay.read(lower_two, row, column, two_columns)
            second_ref[lay.lanes(row), lay.lanes(index)] = block * keep.astype(F32)
    for row in range(level_count):
        for part in range(lay.ratio):
            total = jnp.zeros((lay.width, lay.width), F32)
            for group in range(one_columns // lay.ratio):
                total = total + lay.read(dinv, row, group * lay.ratio + part, one_columns)
            dinv_ref[:, lay.lanes(row * lay.ratio + part)] = total


def fill_panel(piece_refs, panel_ref):
    start = 0
    rows = panel_ref.shape[1]
    for piece_ref in piece_refs:
        place, first = divmod(start, rows)
        panel_ref[place, first : first + piece_ref.shape[0], :] = piece_ref[...]
        start += piece_ref.shape[0]


def panel_columns(lay, panel_ref, rows, source, flip, width):
    place = lax.rem(source, lay.pcol) ^ flip
    start = pl.multiple_of(lax.div(source, lay.pcol) * width, width)
    return panel_ref[place, rows, pl.ds(start, width)]


def gathered_source(lay, place_ref, slot):
    chips = lay.prow // 2
    row = place_ref[0] ^ (slot // chips)
    return lax.rem(row - 2 * (slot % chips) + lay.prow, lay.prow)


def paired_source(lay, place_ref, slot):
    kinds = len(PAIR_FLOWS) + 1
    row = place_ref[0] ^ (slot // kinds)
    kind = slot % kinds
    if kind == 0:
        return row
    plane = lax.div(row, 2)
    source = jnp.int32(0)
    for origin, target in PAIR_FLOWS[kind - 1]:
        source = jnp.where(plane == target, origin, source)
    return source * 2 + lax.rem(row, 2)


def solve_rows(lay, weights, source_of, place_ref, root_ref, slot_refs):
    width = slot_refs[0].shape[0]
    totals = {}
    for slot, slot_ref in enumerate(slot_refs):
        source = source_of(lay, place_ref, slot)
        root_part = panel_columns(lay, root_ref, slice(None), source, 0, width)
        part = product(halves(root_part), halves(slot_ref[...]))
        weight = weights[slot]
        totals[weight] = totals[weight] + part if weight in totals else part
    total = sum(part if weight == 1.0 else part * weight for weight, part in totals.items())
    return total.T


def packed_diagonal(lay, place_ref, segment_ref, left, panel_ref, out_ref, groups, paired):
    rows = out_ref.shape[1]
    depth = left[0].shape[1]
    pcol_place, flip = place_ref[1], place_ref[2]
    for place in range(lay.prow):
        start = (place // lay.pcol) * groups * lay.width
        columns = panel_ref[(place % lay.pcol) ^ flip, :depth, start : start + groups * lay.width]
        result = product(left, halves(columns))
        for index, column in lay.blocks(rows // lay.width):
            node = segment_ref[lay.column_id(column, pcol_place)]
            kept = jnp.zeros((lay.width, lay.width), F32)
            for group in range(groups):
                part = result[lay.lanes(index), lay.lanes(group)]
                same = segment_ref[group * lay.prow + place] == node
                kept = kept + jnp.where(same, part, 0.0)
            target = index
            if paired and place >= lay.pcol:
                target = (index + groups) % (2 * groups)
            out_ref[place, lay.lanes(target), :] = kept


def level_one_kernel(lay, weights, source_of, groups, pieces, place_ref, segment_ref, root_ref, *refs):
    piece_refs, slot_refs = refs[:pieces], refs[pieces:-2]
    out_ref, panel_ref = refs[-2:]
    fill_panel(piece_refs, panel_ref)
    solved = solve_rows(lay, weights, source_of, place_ref, root_ref, slot_refs)
    paired = source_of is paired_source
    packed_diagonal(lay, place_ref, segment_ref, halves(solved), panel_ref, out_ref, groups, paired)


def solve_two_kernel(lay, weights, source_of, place_ref, root_ref, *refs):
    refs[-1][...] = solve_rows(lay, weights, source_of, place_ref, root_ref, refs[:-1])


def keep_columns(lay, place_ref, seg_one, seg_two, parent, level_row, value):
    parts = [None] * (value.shape[1] // lay.width)
    for index, column in lay.blocks(value.shape[1] // lay.width):
        above = parent[seg_two[lay.column_id(column, place_ref[1])]]
        parts[index] = jnp.where(seg_one[level_row] == above, value[:, lay.lanes(index)], 0.0)
    return jnp.concatenate(parts, axis=1)


def level_slot(level_refs, slot):
    half = level_refs[0].shape[0]
    return level_refs[slot // half][slot % half]


def level_two_kernel(lay, weight, groups, level_groups, pieces, place_ref, seg_one, seg_two, parent, solved_ref, *refs):
    level_refs, piece_refs = refs[:2], refs[2 : 2 + pieces]
    out_ref, panel_ref = refs[-2:]
    fill_panel(piece_refs, panel_ref)
    width = lay.width
    depth = solved_ref.shape[1]
    columns = level_refs[0].shape[2]
    total = jnp.zeros((level_groups * width, columns), F32)
    for slot in range(lay.prow):
        source = gathered_source(lay, place_ref, slot)
        place, part = lax.rem(source, lay.pcol) ^ place_ref[2], lax.div(source, lay.pcol)
        dinv_parts = []
        for group in range(level_groups):
            start = pl.multiple_of((group * lay.ratio + part) * width, width)
            dinv_parts.append(panel_ref[place, pl.ds(depth + width, width), pl.ds(start, width)])
        dinv_part = jnp.concatenate(dinv_parts, axis=0)
        total = total + product(halves(dinv_part), halves(level_slot(level_refs, slot)))
    extra = jnp.zeros((width, columns), F32)
    for group in range(level_groups):
        level_row = group * lay.prow + place_ref[0]
        lines = total[lay.lanes(group), :]
        extra = extra + keep_columns(lay, place_ref, seg_one, seg_two, parent, level_row, lines)
    left = jnp.concatenate([solved_ref[...], (extra * weight).T], axis=1)
    packed_diagonal(lay, place_ref, seg_two, halves(left), panel_ref, out_ref, groups, weight != 1.0)


def update_kernel(lay, groups, pieces, place_ref, seg_one, seg_two, parent, lower_ref, dinv_ref, *refs):
    level_refs, piece_refs = refs[:2], refs[2 : 2 + pieces]
    out_ref, bundle_ref, panel_ref = refs[-3:]
    fill_panel(piece_refs, panel_ref)
    width = lay.width
    rows = lower_ref.shape[0]
    total = jnp.zeros(lower_ref.shape, F32)
    for slot in range(lay.prow):
        source = gathered_source(lay, place_ref, slot)
        panel_part = panel_columns(lay, panel_ref, slice(None), source, place_ref[2], groups * width)
        value = level_slot(level_refs, slot)
        parts = [
            keep_columns(lay, place_ref, seg_one, seg_two, parent, group * lay.prow + source, value)
            for group in range(groups)
        ]
        total = total + product(halves(panel_part), halves(jnp.concatenate(parts, axis=0)))
    updated = lower_ref[...] - total
    out_ref[...] = updated
    bundle_ref[:rows, :] = updated
    bundle_ref[rows : rows + width, :] = level_slot(level_refs, 0)
    bundle_ref[rows + width :, :] = dinv_ref[...]


def finish_kernel(lay, count, columns, paired, place_ref, segment_ref, diag_ref, dinv_ref, *refs):
    turned_refs, out_ref = refs[:-1], refs[-1]
    prow_place, pcol_place = place_ref[0], place_ref[1]
    groups = columns // lay.ratio
    upper = lax.div(prow_place, lay.pcol)
    for index, column in lay.blocks(columns):
        start = index * lay.width
        if paired:
            part = (index // groups) ^ upper
            start = pl.multiple_of((part * groups + index % groups) * lay.width, lay.width)
        block = diag_ref[pl.ds(start, lay.width), :].T
        for row in range(count):
            value = block
            if paired:
                lines = lay.lanes(row)
                even, odd = (ref[lines, :] for ref in turned_refs)
                value = block + jnp.where(upper == index // groups, even, odd)
            same = (
                segment_ref[row * lay.prow + prow_place]
                == segment_ref[lay.column_id(column, pcol_place)]
            )
            value = jnp.where(same, lay.read(dinv_ref, row, column, columns) + value, 0.0)
            out_ref[pl.ds(row * lay.width * columns + column, lay.width, stride=columns), :] = value


def shift_rows(piece, pairs):
    return lax.ppermute(
        piece, "prow", [(2 * source + core, 2 * target + core) for source, target in pairs for core in range(2)]
    )


def rotations(piece, prow_total):
    chips = prow_total // 2
    return [
        shift_rows(piece, [(chip, (chip + steps) % chips) for chip in range(chips)])
        for steps in range(1, chips)
    ]


def swap_cores(piece, prow_total):
    return lax.ppermute(piece, "prow", [(place, place ^ 1) for place in range(prow_total)])


PAIR_FLOWS = (((1, 0), (3, 1), (0, 2), (2, 3)), ((2, 1), (0, 3)))


def neighbour(piece, flip, pcol_total):
    return lax.ppermute(piece, "pcol", [(place, place ^ flip) for place in range(pcol_total)])


def tied(*values):
    return lax.optimization_barrier(values)


def on_device(
    root_inverse,
    lower_one,
    lower_two,
    dinv_one,
    dinv_two,
    seg_one,
    seg_two,
    parent_two,
    pattern_one,
    pattern_two,
):
    width = root_inverse.shape[2]
    prow_total = lax.axis_size("prow")
    pcol_total = lax.axis_size("pcol")
    prow_place = lax.axis_index("prow").astype(jnp.int32)
    pcol_place = lax.axis_index("pcol").astype(jnp.int32)
    lay = Layout(prow_total, pcol_total, width)
    root_count, root_columns = root_inverse.shape[0], root_inverse.shape[3]
    level_count, one_columns = dinv_one.shape[0], dinv_one.shape[3]
    second_count, two_columns = dinv_two.shape[0], dinv_two.shape[3]
    root_total = pattern_one.shape[1]
    groups_one, groups_two = one_columns // lay.ratio, two_columns // lay.ratio
    counts = (root_count, level_count, one_columns, two_columns, root_total)
    rows = root_count * width
    paired = prow_total == 8 and pcol_total == 4
    flip = pcol_place if paired else jnp.zeros_like(pcol_place)
    place = jnp.stack([prow_place, pcol_place, flip])

    def lines(argument):
        return argument.reshape(-1, width)

    first, level = vmem_call(
        functools.partial(first_kernel, lay, counts),
        (out_shape(rows, one_columns * width), out_shape(width, two_columns * width)),
        [place, seg_one, seg_two, parent_two, pattern_one, pattern_two],
        [lines(lower_one), lines(lower_two)],
    )
    root = vmem_call(
        functools.partial(root_kernel, lay, root_count, root_columns),
        out_shape(rows, root_columns * width),
        [],
        [lines(root_inverse)],
    )

    root_panel = lax.all_gather(root, "pcol", axis=0, tiled=False)

    def start_panel(piece):
        if paired:
            return [neighbour(piece, 1, pcol_total), neighbour(piece, 2, pcol_total)]
        gathered = lax.all_gather(piece, "pcol", axis=0, tiled=False)
        return [gathered[source] for source in range(pcol_total)]

    def end_panel(piece, started):
        if not paired:
            return started
        beside_x, beside_y = started
        middle = piece.shape[0] // 2
        return [
            piece,
            beside_x,
            beside_y,
            neighbour(beside_y[:middle], 1, pcol_total),
            neighbour(beside_x[middle:], 2, pcol_total),
        ]

    def start_slots(piece):
        if paired:
            return [piece] + [shift_rows(piece, flow) for flow in PAIR_FLOWS]
        return [piece] + rotations(piece, prow_total)

    def both_cores(pieces):
        return pieces + [swap_cores(part, prow_total) for part in pieces]

    source_of = paired_source if paired else gathered_source
    weights = [0.5, 1.0, 1.0] * 2 if paired else [1.0] * prow_total

    first_started = start_panel(first)
    level_pieces = rotations(level, prow_total)
    first_later, level_pieces = tied(first, level_pieces)
    first_slots = start_slots(first_later)
    second_root, dinv_packed, level_own = vmem_call(
        functools.partial(second_kernel, lay, counts),
        (
            out_shape(rows, two_columns * width),
            out_shape(width, level_count * lay.ratio * width),
            out_shape(prow_total // 2, width, two_columns * width),
        ),
        [place, seg_two, parent_two, pattern_one, pattern_two],
        [lines(lower_two), lines(dinv_one), level, *level_pieces],
    )
    level_slots = [level_own, swap_cores(level_own, prow_total)]
    first_pieces = end_panel(first, first_started)
    first_pieces, level_slots, first_slots[:-1] = tied(first_pieces, level_slots, first_slots[:-1])
    first_slots = both_cores(first_slots)

    size = rows * one_columns * width
    bundle_rows = rows + 2 * width
    second, bundle = vmem_call(
        functools.partial(update_kernel, lay, groups_one, len(first_pieces)),
        (out_shape(rows, two_columns * width), out_shape(bundle_rows, two_columns * width)),
        [place, seg_one, seg_two, parent_two],
        [second_root, dinv_packed, *level_slots, *first_pieces],
        [pltpu.VMEM((pcol_total, rows, one_columns * width), F32)],
        flops=6 * size * seg_one.shape[0] * width,
    )
    second_slots = start_slots(second)
    bundle, first_slots = tied(bundle, first_slots)
    bundle_started = start_panel(bundle)
    packed_one = vmem_call(
        functools.partial(level_one_kernel, lay, weights, source_of, groups_one, len(first_pieces)),
        out_shape(prow_total, one_columns * width, width),
        [place, seg_one],
        [root_panel, *first_pieces, *first_slots],
        [pltpu.VMEM((pcol_total, rows, one_columns * width), F32)],
        flops=6 * size * (root_total + seg_one.shape[0]) * width,
        after=[second],
    )
    packed_one, second_slots, bundle_started = tied(packed_one, second_slots, bundle_started)
    second_slots = both_cores(second_slots)
    diag_one = lax.psum_scatter(packed_one, "prow", scatter_dimension=0, tiled=False)
    bundle_pieces = end_panel(bundle, bundle_started)
    solved_two = vmem_call(
        functools.partial(solve_two_kernel, lay, weights, source_of),
        out_shape(two_columns * width, rows),
        [place],
        [root_panel, *second_slots],
        flops=6 * size * root_total * width,
    )
    packed_two = vmem_call(
        functools.partial(level_two_kernel, lay, weights[0], groups_two, level_count, len(bundle_pieces)),
        out_shape(prow_total, two_columns * width, width),
        [place, seg_one, seg_two, parent_two],
        [solved_two, *level_slots, *bundle_pieces],
        [pltpu.VMEM((pcol_total, bundle_rows, two_columns * width), F32)],
        flops=6 * size * seg_two.shape[0] * width,
    )
    diag_two = lax.psum_scatter(packed_two, "prow", scatter_dimension=0, tiled=False)

    def partners(diag, groups):
        turned = []
        for turn in range(lay.ratio):
            pairs = []
            for row in range(prow_total):
                part = (row // pcol_total) ^ turn
                for column in range(pcol_total):
                    target = (column + pcol_total * part) * pcol_total + row % pcol_total
                    pairs.append((row * pcol_total + column, target))
            sent = diag[turn * groups * width : (turn + 1) * groups * width]
            turned.append(lax.ppermute(sent, BOTH, pairs))
        return turned

    def finish(dinv, diag, segments, groups):
        count, columns = dinv.shape[0], dinv.shape[3]
        result = vmem_call(
            functools.partial(finish_kernel, lay, count, columns, paired),
            out_shape(count * width * columns, width),
            [place, segments],
            [diag, lines(dinv)] + (partners(diag, groups) if paired else []),
        )
        return result.reshape(dinv.shape)

    return (
        finish(dinv_one, diag_one, seg_one, groups_one),
        finish(dinv_two, diag_two, seg_two, groups_two),
    )


def solution(mesh):
    cyclic = P(None, "prow", None, None, "pcol", None)
    return jax.shard_map(
        on_device,
        mesh=mesh,
        in_specs=(cyclic,) * 5 + (P(),) * 5,
        out_specs=(cyclic, cyclic),
        check_vma=False,
    )
```

```python
import functools

import jax
import jax.numpy as jnp
from jax import lax
from jax.experimental import pallas as pl
from jax.experimental.pallas import tpu as pltpu
from jax.sharding import PartitionSpec as P

VMEM_LIMIT = 56 * 1024 * 1024
F32 = jnp.float32
BOTH = ("prow", "pcol")


def halves(value):
    high = value.astype(jnp.bfloat16)
    low = (value - high.astype(F32)).astype(jnp.bfloat16)
    return high, low


def product(left, right):
    left_high, left_low = left
    right_high, right_low = right
    dot = functools.partial(jnp.dot, preferred_element_type=F32)
    return dot(left_high, right_high) + (dot(left_high, right_low) + dot(left_low, right_high))


def vmem_call(kernel, outs, smem_args, vmem_args, any_args=(), scratch=(), flops=0, after=()):
    def body(*refs):
        kernel(*refs[len(after) :])

    return pl.pallas_call(
        body,
        out_shape=outs,
        in_specs=[pl.BlockSpec(memory_space=pl.ANY)] * len(after)
        + [pl.BlockSpec(memory_space=pltpu.SMEM)] * len(smem_args)
        + [pl.BlockSpec(memory_space=pltpu.VMEM)] * len(vmem_args)
        + [pl.BlockSpec(memory_space=pl.ANY)] * len(any_args),
        out_specs=jax.tree.map(lambda _: pl.BlockSpec(memory_space=pltpu.VMEM), outs),
        scratch_shapes=scratch,
        compiler_params=pltpu.CompilerParams(vmem_limit_bytes=VMEM_LIMIT),
        cost_estimate=pl.CostEstimate(
            flops=flops,
            bytes_accessed=sum(4 * arg.size for arg in (*vmem_args, *any_args)),
            transcendentals=0,
        ),
    )(*after, *smem_args, *vmem_args, *any_args)


def out_shape(*dims):
    return jax.ShapeDtypeStruct(dims, F32)


class Layout:
    def __init__(self, prow, pcol, width):
        self.prow, self.pcol, self.width = prow, pcol, width
        self.ratio = prow // pcol

    def blocks(self, columns):
        for part in range(self.ratio):
            for group in range(columns // self.ratio):
                yield part * (columns // self.ratio) + group, group * self.ratio + part

    def column_id(self, column, pcol_place):
        return column * self.pcol + pcol_place

    def read(self, ref, row, column, columns):
        return ref[pl.ds(row * self.width * columns + column, self.width, stride=columns), :]

    def lanes(self, index):
        return slice(index * self.width, (index + 1) * self.width)


def first_kernel(lay, counts, place_ref, seg_one, seg_two, parent, one, two, lower_one, lower_two, *outs):
    first_ref, level_ref = outs
    root_count, level_count, one_columns, two_columns, root_total = counts
    prow_place, pcol_place = place_ref[0], place_ref[1]
    for index, column in lay.blocks(one_columns):
        node = seg_one[lay.column_id(column, pcol_place)]
        for row in range(root_count):
            keep = one[node, row * lay.prow + prow_place]
            block = lay.read(lower_one, row, column, one_columns)
            first_ref[lay.lanes(row), lay.lanes(index)] = block * keep.astype(F32)
    for index, column in lay.blocks(two_columns):
        node = seg_two[lay.column_id(column, pcol_place)]
        above = parent[node]
        total = jnp.zeros((lay.width, lay.width), F32)
        for row in range(level_count):
            level_row = row * lay.prow + prow_place
            keep = jnp.where(seg_one[level_row] == above, two[node, root_total + level_row], 0)
            block = lay.read(lower_two, root_count + row, column, two_columns)
            total = total + block * keep.astype(F32)
        level_ref[:, lay.lanes(index)] = total


def root_kernel(lay, root_count, root_columns, root, root_ref):
    for index, column in lay.blocks(root_columns):
        for row in range(root_count):
            block = lay.read(root, row, column, root_columns)
            root_ref[lay.lanes(row), lay.lanes(index)] = block


def second_kernel(lay, counts, place_ref, seg_two, parent, one, two, lower_two, dinv, *refs):
    root_count, level_count, one_columns, two_columns, root_total = counts
    level_refs = refs[:-3]
    second_ref, dinv_ref, stack_ref = refs[-3:]
    for row in range(level_count):
        for part in range(lay.ratio):
            total = jnp.zeros((lay.width, lay.width), F32)
            for group in range(one_columns // lay.ratio):
                total = total + lay.read(dinv, row, group * lay.ratio + part, one_columns)
            dinv_ref[:, lay.lanes(row * lay.ratio + part)] = total
    for slot, level_ref in enumerate(level_refs):
        stack_ref[slot] = level_ref[...]
    prow_place, pcol_place = place_ref[0], place_ref[1]
    for index, column in lay.blocks(two_columns):
        node = seg_two[lay.column_id(column, pcol_place)]
        above = parent[node]
        for row in range(root_count):
            root_row = row * lay.prow + prow_place
            keep = two[node, root_row] * one[above, root_row]
            block = lay.read(lower_two, row, column, two_columns)
            second_ref[lay.lanes(row), lay.lanes(index)] = block * keep.astype(F32)


def start_fill(piece_refs, panel_ref, sem_ref):
    start = 0
    rows = panel_ref.shape[1]
    copies = []
    for index, piece_ref in enumerate(piece_refs):
        place, first = divmod(start, rows)
        lines = pl.ds(first, piece_ref.shape[0])
        copy = pltpu.make_async_copy(piece_ref, panel_ref.at[place, lines, :], sem_ref.at[index])
        copy.start()
        copies.append(copy)
        start += piece_ref.shape[0]
    return copies


def panel_columns(lay, panel_ref, rows, source, flip, width):
    place = lax.rem(source, lay.pcol) ^ flip
    start = pl.multiple_of(lax.div(source, lay.pcol) * width, width)
    return panel_ref[place, rows, pl.ds(start, width)]


def gathered_source(lay, place_ref, slot):
    chips = lay.prow // 2
    row = place_ref[0] ^ (slot // chips)
    return lax.rem(row - 2 * (slot % chips) + lay.prow, lay.prow)


def paired_source(lay, place_ref, slot):
    kinds = len(PAIR_FLOWS) + 1
    row = place_ref[0] ^ (slot // kinds)
    kind = slot % kinds
    if kind == 0:
        return row
    plane = lax.div(row, 2)
    source = jnp.int32(0)
    for origin, target in PAIR_FLOWS[kind - 1]:
        source = jnp.where(plane == target, origin, source)
    return source * 2 + lax.rem(row, 2)


def start_solve(lay, source_of, place_ref, root_ref, slot_refs, block_ref, held_ref, sem_ref):
    width = slot_refs[0].shape[0]
    copies = []
    for slot, slot_ref in enumerate(slot_refs):
        source = source_of(lay, place_ref, slot)
        start = pl.multiple_of(lax.div(source, lay.pcol) * width, width)
        columns = root_ref.at[lax.rem(source, lay.pcol), :, pl.ds(start, width)]
        pair = (
            pltpu.make_async_copy(columns, block_ref.at[slot], sem_ref.at[2 * slot]),
            pltpu.make_async_copy(slot_ref, held_ref.at[slot], sem_ref.at[2 * slot + 1]),
        )
        for copy in pair:
            copy.start()
        copies.append(pair)
    return copies


def solve_rows(weights, copies, block_ref, held_ref):
    totals = {}
    for slot, pair in enumerate(copies):
        for copy in pair:
            copy.wait()
        part = product(halves(block_ref[slot]), halves(held_ref[slot]))
        weight = weights[slot]
        totals[weight] = totals[weight] + part if weight in totals else part
    total = sum(part if weight == 1.0 else part * weight for weight, part in totals.items())
    return total.T


def solve_scratch(slots, rows, width, columns):
    return [
        pltpu.VMEM((slots, rows, width), F32),
        pltpu.VMEM((slots, width, columns), F32),
        pltpu.SemaphoreType.DMA((2 * slots,)),
    ]


def panel_scratch(pieces, places, rows, columns):
    return [pltpu.VMEM((places, rows, columns), F32), pltpu.SemaphoreType.DMA((pieces,))]


def packed_diagonal(lay, place_ref, segment_ref, left, panel_ref, out_ref, groups, paired):
    rows = out_ref.shape[1]
    depth = left[0].shape[1]
    pcol_place, flip = place_ref[1], place_ref[2]
    for place in range(lay.prow):
        part = place // lay.pcol
        start = part * groups * lay.width
        columns = panel_ref[(place % lay.pcol) ^ flip, :depth, start : start + groups * lay.width]
        result = product(left, halves(columns))
        for index, column in lay.blocks(rows // lay.width):
            node = segment_ref[lay.column_id(column, pcol_place)]
            kept = jnp.zeros((lay.width, lay.width), F32)
            for group in range(groups):
                same = segment_ref[group * lay.prow + place] == node
                kept = kept + jnp.where(same, result[lay.lanes(index), lay.lanes(group)], 0.0)
            target = (index + groups) % (2 * groups) if paired and part else index
            out_ref[place, lay.lanes(target), :] = kept


def level_one_kernel(lay, weights, source_of, groups, pieces, place_ref, segment_ref, root_ref, *refs):
    piece_refs, slot_refs = refs[:pieces], refs[pieces : pieces + len(weights)]
    out_ref, panel_ref, panel_sem, block_ref, held_ref, sem_ref = refs[pieces + len(weights) :]
    copies = start_solve(lay, source_of, place_ref, root_ref, slot_refs, block_ref, held_ref, sem_ref)
    fills = start_fill(piece_refs, panel_ref, panel_sem)
    left = halves(solve_rows(weights, copies, block_ref, held_ref))
    for copy in fills:
        copy.wait()
    paired = source_of is paired_source
    packed_diagonal(lay, place_ref, segment_ref, left, panel_ref, out_ref, groups, paired)


def solve_two_kernel(lay, weights, source_of, place_ref, root_ref, *refs):
    slot_refs = refs[: len(weights)]
    out_ref, block_ref, held_ref, sem_ref = refs[len(weights) :]
    copies = start_solve(lay, source_of, place_ref, root_ref, slot_refs, block_ref, held_ref, sem_ref)
    out_ref[...] = solve_rows(weights, copies, block_ref, held_ref)


def keep_columns(lay, place_ref, seg_one, seg_two, parent, level_row, value):
    parts = [None] * (value.shape[1] // lay.width)
    for index, column in lay.blocks(value.shape[1] // lay.width):
        above = parent[seg_two[lay.column_id(column, place_ref[1])]]
        parts[index] = jnp.where(seg_one[level_row] == above, value[:, lay.lanes(index)], 0.0)
    return jnp.concatenate(parts, axis=1)


def level_slot(level_refs, slot):
    half = level_refs[0].shape[0]
    return level_refs[slot // half][slot % half]


def level_two_kernel(lay, paired, weight, groups, level_groups, place_ref, seg_one, seg_two, parent, *refs):
    pieces = refs[-1].shape[0]
    solved_ref, level_refs, piece_refs = refs[0], refs[1:3], refs[3 : 3 + pieces]
    out_ref, panel_ref, panel_sem = refs[-3:]
    fills = start_fill(piece_refs, panel_ref, panel_sem)
    width = lay.width
    depth = solved_ref.shape[1]
    columns = level_refs[0].shape[2]
    solved = solved_ref[...]
    for copy in fills:
        copy.wait()
    packed = jnp.zeros((level_groups * width, columns), F32)
    for slot in range(lay.prow):
        source = gathered_source(lay, place_ref, slot)
        place, part = lax.rem(source, lay.pcol) ^ place_ref[2], lax.div(source, lay.pcol)
        dinv_parts = []
        for group in range(level_groups):
            start = pl.multiple_of((group * lay.ratio + part) * width, width)
            dinv_parts.append(panel_ref[place, pl.ds(depth + width, width), pl.ds(start, width)])
        dinv_part = jnp.concatenate(dinv_parts, axis=0)
        packed = packed + product(halves(dinv_part), halves(level_slot(level_refs, slot)))
    extra = jnp.zeros((width, columns), F32)
    for group in range(level_groups):
        level_row = group * lay.prow + place_ref[0]
        lines = packed[lay.lanes(group), :]
        extra = extra + keep_columns(lay, place_ref, seg_one, seg_two, parent, level_row, lines)
    left = halves(jnp.concatenate([solved, (extra * weight).T], axis=1))
    packed_diagonal(lay, place_ref, seg_two, left, panel_ref, out_ref, groups, paired)


def update_kernel(lay, groups, place_ref, seg_one, seg_two, parent, lower_ref, dinv_ref, *refs):
    pieces = refs[-1].shape[0]
    level_refs, piece_refs = refs[:2], refs[2 : 2 + pieces]
    out_ref, bundle_ref, panel_ref, panel_sem = refs[2 + pieces :]
    fills = start_fill(piece_refs, panel_ref, panel_sem)
    width = lay.width
    rows = lower_ref.shape[0]
    total = jnp.zeros(lower_ref.shape, F32)
    for copy in fills:
        copy.wait()
    for slot in range(lay.prow):
        source = gathered_source(lay, place_ref, slot)
        panel_part = panel_columns(lay, panel_ref, slice(None), source, place_ref[2], groups * width)
        value = level_slot(level_refs, slot)
        parts = [
            keep_columns(lay, place_ref, seg_one, seg_two, parent, group * lay.prow + source, value)
            for group in range(groups)
        ]
        total = total + product(halves(panel_part), halves(jnp.concatenate(parts, axis=0)))
    updated = lower_ref[...] - total
    out_ref[...] = updated
    bundle_ref[:rows, :] = updated
    bundle_ref[rows : rows + width, :] = level_slot(level_refs, 0)
    bundle_ref[rows + width :, :] = dinv_ref[...]


def finish_kernel(lay, count, place_ref, segment_ref, diag_ref, dinv_ref, *refs):
    turned_refs, out_ref = refs[:-1], refs[-1]
    prow_place, pcol_place = place_ref[0], place_ref[1]
    columns = diag_ref.shape[0] // lay.width
    groups = columns // lay.ratio
    upper = lax.div(prow_place, lay.pcol)
    for index, column in lay.blocks(columns):
        start = index * lay.width
        if turned_refs:
            part = (index // groups) ^ upper
            start = pl.multiple_of((part * groups + index % groups) * lay.width, lay.width)
        block = diag_ref[pl.ds(start, lay.width), :].T
        for row in range(count):
            value = block
            if turned_refs:
                even, odd = (ref[lay.lanes(row), :] for ref in turned_refs)
                value = block + jnp.where(upper == index // groups, even, odd)
            same = (
                segment_ref[row * lay.prow + prow_place]
                == segment_ref[lay.column_id(column, pcol_place)]
            )
            value = jnp.where(same, lay.read(dinv_ref, row, column, columns) + value, 0.0)
            out_ref[pl.ds(row * lay.width * columns + column, lay.width, stride=columns), :] = value


def shift_rows(piece, pairs):
    return lax.ppermute(
        piece, "prow", [(2 * source + core, 2 * target + core) for source, target in pairs for core in range(2)]
    )


def rotations(piece, prow_total):
    chips = prow_total // 2
    return [
        shift_rows(piece, [(chip, (chip + steps) % chips) for chip in range(chips)])
        for steps in range(1, chips)
    ]


def swap_cores(piece, prow_total):
    return lax.ppermute(piece, "prow", [(place, place ^ 1) for place in range(prow_total)])


PAIR_FLOWS = (((1, 0), (3, 1), (0, 2), (2, 3)), ((2, 1), (0, 3)))


def neighbour(piece, flip, pcol_total):
    return lax.ppermute(piece, "pcol", [(place, place ^ flip) for place in range(pcol_total)])


def tied(*values):
    return lax.optimization_barrier(values)


def on_device(
    root_inverse,
    lower_one,
    lower_two,
    dinv_one,
    dinv_two,
    seg_one,
    seg_two,
    parent_two,
    pattern_one,
    pattern_two,
):
    width = root_inverse.shape[2]
    prow_total = lax.axis_size("prow")
    pcol_total = lax.axis_size("pcol")
    prow_place = lax.axis_index("prow").astype(jnp.int32)
    pcol_place = lax.axis_index("pcol").astype(jnp.int32)
    lay = Layout(prow_total, pcol_total, width)
    root_count, root_columns = root_inverse.shape[0], root_inverse.shape[3]
    level_count, one_columns = dinv_one.shape[0], dinv_one.shape[3]
    second_count, two_columns = dinv_two.shape[0], dinv_two.shape[3]
    root_total = pattern_one.shape[1]
    groups_one, groups_two = one_columns // lay.ratio, two_columns // lay.ratio
    counts = (root_count, level_count, one_columns, two_columns, root_total)
    rows = root_count * width
    paired = prow_total == 8 and pcol_total == 4
    flip = pcol_place if paired else jnp.zeros_like(pcol_place)
    place = jnp.stack([prow_place, pcol_place, flip])

    def lines(argument):
        return argument.reshape(-1, width)

    first, level = vmem_call(
        functools.partial(first_kernel, lay, counts),
        (out_shape(rows, one_columns * width), out_shape(width, two_columns * width)),
        [place, seg_one, seg_two, parent_two, pattern_one, pattern_two],
        [lines(lower_one), lines(lower_two)],
    )
    root = vmem_call(
        functools.partial(root_kernel, lay, root_count, root_columns),
        out_shape(rows, root_columns * width),
        [],
        [lines(root_inverse)],
    )

    root_panel = lax.all_gather(root, "pcol", axis=0, tiled=False)

    def start_panel(piece):
        if paired:
            return [neighbour(piece, 1, pcol_total), neighbour(piece, 2, pcol_total)]
        gathered = lax.all_gather(piece, "pcol", axis=0, tiled=False)
        return [gathered[source] for source in range(pcol_total)]

    def end_panel(piece, started):
        if not paired:
            return started
        beside_x, beside_y = started
        middle = piece.shape[0] // 2
        return [
            piece,
            beside_x,
            beside_y,
            neighbour(beside_y[:middle], 1, pcol_total),
            neighbour(beside_x[middle:], 2, pcol_total),
        ]

    def start_slots(piece):
        if paired:
            return [piece] + [shift_rows(piece, flow) for flow in PAIR_FLOWS]
        return [piece] + rotations(piece, prow_total)

    def both_cores(pieces):
        return pieces + [swap_cores(part, prow_total) for part in pieces]

    source_of = paired_source if paired else gathered_source
    weights = [0.5, 1.0, 1.0] * 2 if paired else [1.0] * prow_total

    first_started = start_panel(first)
    level_pieces = rotations(level, prow_total)
    first_later, level_pieces = tied(first, level_pieces)
    first_slots = start_slots(first_later)
    second_root, dinv_packed, level_own = vmem_call(
        functools.partial(second_kernel, lay, counts),
        (
            out_shape(rows, two_columns * width),
            out_shape(width, level_count * lay.ratio * width),
            out_shape(prow_total // 2, width, two_columns * width),
        ),
        [place, seg_two, parent_two, pattern_one, pattern_two],
        [lines(lower_two), lines(dinv_one), level, *level_pieces],
    )
    level_slots = [level_own, swap_cores(level_own, prow_total)]
    first_pieces = end_panel(first, first_started)
    first_pieces, level_slots, first_slots[:-1] = tied(first_pieces, level_slots, first_slots[:-1])
    first_slots = both_cores(first_slots)

    size = rows * one_columns * width
    bundle_rows = rows + 2 * width
    pieces = len(first_pieces)
    second, bundle = vmem_call(
        functools.partial(update_kernel, lay, groups_one),
        (out_shape(rows, two_columns * width), out_shape(bundle_rows, two_columns * width)),
        [place, seg_one, seg_two, parent_two],
        [second_root, dinv_packed, *level_slots],
        first_pieces,
        panel_scratch(pieces, pcol_total, rows, one_columns * width),
        flops=6 * size * seg_one.shape[0] * width,
    )
    second_slots = start_slots(second)
    bundle, first_slots = tied(bundle, first_slots)
    bundle_started = start_panel(bundle)
    packed_one = vmem_call(
        functools.partial(level_one_kernel, lay, weights, source_of, groups_one, pieces),
        out_shape(prow_total, one_columns * width, width),
        [place, seg_one],
        [],
        [root_panel, *first_pieces, *first_slots],
        panel_scratch(pieces, pcol_total, rows, one_columns * width)
        + solve_scratch(len(weights), rows, rows, one_columns * width),
        flops=6 * size * (root_total + seg_one.shape[0]) * width,
        after=[second],
    )
    packed_one, second_slots, bundle_started = tied(packed_one, second_slots, bundle_started)
    second_slots = both_cores(second_slots)
    diag_one = lax.psum_scatter(packed_one, "prow", scatter_dimension=0, tiled=False)
    bundle_pieces = end_panel(bundle, bundle_started)
    solved_two = vmem_call(
        functools.partial(solve_two_kernel, lay, weights, source_of),
        out_shape(two_columns * width, rows),
        [place],
        [],
        [root_panel, *second_slots],
        solve_scratch(len(weights), rows, rows, two_columns * width),
        flops=6 * size * root_total * width,
    )
    packed_two = vmem_call(
        functools.partial(level_two_kernel, lay, paired, weights[0], groups_two, level_count),
        out_shape(prow_total, two_columns * width, width),
        [place, seg_one, seg_two, parent_two],
        [solved_two, *level_slots],
        bundle_pieces,
        panel_scratch(pieces, pcol_total, bundle_rows, two_columns * width),
        flops=6 * size * seg_two.shape[0] * width,
    )

    diag_two = lax.psum_scatter(packed_two, "prow", scatter_dimension=0, tiled=False)

    def partners(diag, groups):
        turned = []
        for turn in range(lay.ratio):
            pairs = []
            for row in range(prow_total):
                part = (row // pcol_total) ^ turn
                for column in range(pcol_total):
                    target = (column + pcol_total * part) * pcol_total + row % pcol_total
                    pairs.append((row * pcol_total + column, target))
            sent = diag[turn * groups * width : (turn + 1) * groups * width]
            turned.append(lax.ppermute(sent, BOTH, pairs))
        return turned

    def finish(dinv, diag, segments, groups):
        count, columns = dinv.shape[0], dinv.shape[3]
        result = vmem_call(
            functools.partial(finish_kernel, lay, count),
            out_shape(count * width * columns, width),
            [place, segments],
            [diag, lines(dinv)] + (partners(diag, groups) if paired else []),
        )
        return result.reshape(dinv.shape)

    return (
        finish(dinv_one, diag_one, seg_one, groups_one),
        finish(dinv_two, diag_two, seg_two, groups_two),
    )


def solution(mesh):
    cyclic = P(None, "prow", None, None, "pcol", None)
    return jax.shard_map(
        on_device,
        mesh=mesh,
        in_specs=(cyclic,) * 5 + (P(),) * 5,
        out_specs=(cyclic, cyclic),
        check_vma=False,
    )
```

```python
import functools

import jax
import jax.numpy as jnp
from jax import lax
from jax.experimental import pallas as pl
from jax.experimental.pallas import tpu as pltpu
from jax.sharding import PartitionSpec as P

VMEM_LIMIT = 56 * 1024 * 1024
F32 = jnp.float32
BOTH = ("prow", "pcol")


def halves(value):
    high = value.astype(jnp.bfloat16)
    low = (value - high.astype(F32)).astype(jnp.bfloat16)
    return high, low


def product(left, right):
    left_high, left_low = left
    right_high, right_low = right
    dot = functools.partial(jnp.dot, preferred_element_type=F32)
    return dot(left_high, right_high) + (dot(left_high, right_low) + dot(left_low, right_high))


def vmem_call(kernel, outs, smem_args, vmem_args, any_args=(), scratch=(), flops=0, after=()):
    def body(*refs):
        kernel(*refs[len(after) :])

    return pl.pallas_call(
        body,
        out_shape=outs,
        in_specs=[pl.BlockSpec(memory_space=pl.ANY)] * len(after)
        + [pl.BlockSpec(memory_space=pltpu.SMEM)] * len(smem_args)
        + [pl.BlockSpec(memory_space=pltpu.VMEM)] * len(vmem_args)
        + [pl.BlockSpec(memory_space=pl.ANY)] * len(any_args),
        out_specs=jax.tree.map(lambda _: pl.BlockSpec(memory_space=pltpu.VMEM), outs),
        scratch_shapes=scratch,
        compiler_params=pltpu.CompilerParams(vmem_limit_bytes=VMEM_LIMIT),
        cost_estimate=pl.CostEstimate(
            flops=flops,
            bytes_accessed=sum(4 * arg.size for arg in (*vmem_args, *any_args)),
            transcendentals=0,
        ),
    )(*after, *smem_args, *vmem_args, *any_args)


def out_shape(*dims):
    return jax.ShapeDtypeStruct(dims, F32)


class Layout:
    def __init__(self, prow, pcol, width):
        self.prow, self.pcol, self.width = prow, pcol, width
        self.ratio = prow // pcol

    def blocks(self, columns):
        for part in range(self.ratio):
            for group in range(columns // self.ratio):
                yield part * (columns // self.ratio) + group, group * self.ratio + part

    def column_id(self, column, pcol_place):
        return column * self.pcol + pcol_place

    def read(self, ref, row, column, columns):
        return ref[pl.ds(row * self.width * columns + column, self.width, stride=columns), :]

    def lanes(self, index):
        return slice(index * self.width, (index + 1) * self.width)


def first_kernel(lay, counts, place_ref, seg_one, seg_two, parent, one, two, lower_one, lower_two, *outs):
    first_ref, level_ref = outs
    root_count, level_count, one_columns, two_columns, root_total = counts
    prow_place, pcol_place = place_ref[0], place_ref[1]
    for index, column in lay.blocks(one_columns):
        node = seg_one[lay.column_id(column, pcol_place)]
        for row in range(root_count):
            keep = one[node, row * lay.prow + prow_place]
            block = lay.read(lower_one, row, column, one_columns)
            first_ref[lay.lanes(row), lay.lanes(index)] = block * keep.astype(F32)
    for index, column in lay.blocks(two_columns):
        node = seg_two[lay.column_id(column, pcol_place)]
        above = parent[node]
        total = jnp.zeros((lay.width, lay.width), F32)
        for row in range(level_count):
            level_row = row * lay.prow + prow_place
            keep = jnp.where(seg_one[level_row] == above, two[node, root_total + level_row], 0)
            block = lay.read(lower_two, root_count + row, column, two_columns)
            total = total + block * keep.astype(F32)
        level_ref[:, lay.lanes(index)] = total


def root_kernel(lay, root_count, root_columns, root, root_ref):
    for index, column in lay.blocks(root_columns):
        for row in range(root_count):
            block = lay.read(root, row, column, root_columns)
            root_ref[lay.lanes(row), lay.lanes(index)] = block


def second_kernel(lay, counts, place_ref, seg_two, parent, one, two, lower_two, dinv, *refs):
    root_count, level_count, one_columns, two_columns, root_total = counts
    level_refs = refs[:-3]
    second_ref, dinv_ref, stack_ref = refs[-3:]
    for row in range(level_count):
        for part in range(lay.ratio):
            total = jnp.zeros((lay.width, lay.width), F32)
            for group in range(one_columns // lay.ratio):
                total = total + lay.read(dinv, row, group * lay.ratio + part, one_columns)
            dinv_ref[:, lay.lanes(row * lay.ratio + part)] = total
    for slot, level_ref in enumerate(level_refs):
        stack_ref[slot] = level_ref[...]
    prow_place, pcol_place = place_ref[0], place_ref[1]
    for index, column in lay.blocks(two_columns):
        node = seg_two[lay.column_id(column, pcol_place)]
        above = parent[node]
        for row in range(root_count):
            root_row = row * lay.prow + prow_place
            keep = two[node, root_row] * one[above, root_row]
            block = lay.read(lower_two, row, column, two_columns)
            second_ref[lay.lanes(row), lay.lanes(index)] = block * keep.astype(F32)


def start_fill(piece_refs, panel_ref, sem_ref):
    start = 0
    rows = panel_ref.shape[1]
    copies = []
    for index, piece_ref in enumerate(piece_refs):
        place, first = divmod(start, rows)
        lines = pl.ds(first, piece_ref.shape[0])
        copy = pltpu.make_async_copy(piece_ref, panel_ref.at[place, lines, :], sem_ref.at[index])
        copy.start()
        copies.append(copy)
        start += piece_ref.shape[0]
    return copies


def panel_columns(lay, panel_ref, rows, source, flip, width):
    place = lax.rem(source, lay.pcol) ^ flip
    start = pl.multiple_of(lax.div(source, lay.pcol) * width, width)
    return panel_ref[place, rows, pl.ds(start, width)]


def gathered_source(lay, place_ref, slot):
    chips = lay.prow // 2
    row = place_ref[0] ^ (slot // chips)
    return lax.rem(row - 2 * (slot % chips) + lay.prow, lay.prow)


def paired_source(lay, place_ref, slot):
    kinds = len(PAIR_FLOWS) + 1
    row = place_ref[0] ^ (slot // kinds)
    kind = slot % kinds
    if kind == 0:
        return row
    plane = lax.div(row, 2)
    source = jnp.int32(0)
    for origin, target in PAIR_FLOWS[kind - 1]:
        source = jnp.where(plane == target, origin, source)
    return source * 2 + lax.rem(row, 2)


def start_solve(lay, source_of, place_ref, root_ref, slot_refs, block_ref, held_ref, sem_ref):
    width = slot_refs[0].shape[0]
    copies = []
    for slot, slot_ref in enumerate(slot_refs):
        source = source_of(lay, place_ref, slot)
        start = pl.multiple_of(lax.div(source, lay.pcol) * width, width)
        columns = root_ref.at[lax.rem(source, lay.pcol), :, pl.ds(start, width)]
        pair = (
            pltpu.make_async_copy(columns, block_ref.at[slot], sem_ref.at[2 * slot]),
            pltpu.make_async_copy(slot_ref, held_ref.at[slot], sem_ref.at[2 * slot + 1]),
        )
        for copy in pair:
            copy.start()
        copies.append(pair)
    return copies


def solve_rows(weights, copies, block_ref, held_ref):
    totals = {}
    for slot, pair in enumerate(copies):
        for copy in pair:
            copy.wait()
        part = product(halves(block_ref[slot]), halves(held_ref[slot]))
        weight = weights[slot]
        totals[weight] = totals[weight] + part if weight in totals else part
    total = sum(part if weight == 1.0 else part * weight for weight, part in totals.items())
    return total.T


def solve_scratch(slots, rows, width, columns):
    return [
        pltpu.VMEM((slots, rows, width), F32),
        pltpu.VMEM((slots, width, columns), F32),
        pltpu.SemaphoreType.DMA((2 * slots,)),
    ]


def panel_scratch(pieces, places, rows, columns):
    return [pltpu.VMEM((places, rows, columns), F32), pltpu.SemaphoreType.DMA((pieces,))]


def packed_diagonal(lay, place_ref, segment_ref, left, panel_ref, out_ref, groups, paired):
    rows = out_ref.shape[1]
    depth = left[0].shape[1]
    pcol_place, flip = place_ref[1], place_ref[2]
    for place in range(lay.prow):
        part = place // lay.pcol
        start = part * groups * lay.width
        columns = panel_ref[(place % lay.pcol) ^ flip, :depth, start : start + groups * lay.width]
        result = product(left, halves(columns))
        for index, column in lay.blocks(rows // lay.width):
            node = segment_ref[lay.column_id(column, pcol_place)]
            kept = jnp.zeros((lay.width, lay.width), F32)
            for group in range(groups):
                same = segment_ref[group * lay.prow + place] == node
                kept = kept + jnp.where(same, result[lay.lanes(index), lay.lanes(group)], 0.0)
            target = (index + groups) % (2 * groups) if paired and part else index
            out_ref[place, lay.lanes(target), :] = kept


def level_one_kernel(lay, weights, source_of, groups, pieces, place_ref, segment_ref, root_ref, *refs):
    piece_refs, slot_refs = refs[:pieces], refs[pieces : pieces + len(weights)]
    out_ref, panel_ref, panel_sem, block_ref, held_ref, sem_ref = refs[pieces + len(weights) :]
    copies = start_solve(lay, source_of, place_ref, root_ref, slot_refs, block_ref, held_ref, sem_ref)
    fills = start_fill(piece_refs, panel_ref, panel_sem)
    left = halves(solve_rows(weights, copies, block_ref, held_ref))
    for copy in fills:
        copy.wait()
    paired = source_of is paired_source
    packed_diagonal(lay, place_ref, segment_ref, left, panel_ref, out_ref, groups, paired)


def solve_two_kernel(lay, weights, source_of, place_ref, root_ref, *refs):
    slot_refs = refs[: len(weights)]
    out_ref, block_ref, held_ref, sem_ref = refs[len(weights) :]
    copies = start_solve(lay, source_of, place_ref, root_ref, slot_refs, block_ref, held_ref, sem_ref)
    out_ref[...] = solve_rows(weights, copies, block_ref, held_ref)


def keep_columns(lay, place_ref, seg_one, seg_two, parent, level_row, value):
    parts = [None] * (value.shape[1] // lay.width)
    for index, column in lay.blocks(value.shape[1] // lay.width):
        above = parent[seg_two[lay.column_id(column, place_ref[1])]]
        parts[index] = jnp.where(seg_one[level_row] == above, value[:, lay.lanes(index)], 0.0)
    return jnp.concatenate(parts, axis=1)


def level_slot(level_refs, slot):
    half = level_refs[0].shape[0]
    return level_refs[slot // half][slot % half]


def level_two_kernel(lay, paired, weight, groups, level_groups, place_ref, seg_one, seg_two, parent, *refs):
    pieces = refs[-1].shape[0]
    solved_ref, level_refs, piece_refs = refs[0], refs[1:3], refs[3 : 3 + pieces]
    out_ref, panel_ref, panel_sem = refs[-3:]
    fills = start_fill(piece_refs, panel_ref, panel_sem)
    width = lay.width
    depth = solved_ref.shape[1]
    columns = level_refs[0].shape[2]
    solved = solved_ref[...]
    for copy in fills:
        copy.wait()
    packed = jnp.zeros((level_groups * width, columns), F32)
    for slot in range(lay.prow):
        source = gathered_source(lay, place_ref, slot)
        place, part = lax.rem(source, lay.pcol) ^ place_ref[2], lax.div(source, lay.pcol)
        dinv_parts = []
        for group in range(level_groups):
            start = pl.multiple_of((group * lay.ratio + part) * width, width)
            dinv_parts.append(panel_ref[place, pl.ds(depth + width, width), pl.ds(start, width)])
        dinv_part = jnp.concatenate(dinv_parts, axis=0)
        packed = packed + product(halves(dinv_part), halves(level_slot(level_refs, slot)))
    extra = jnp.zeros((width, columns), F32)
    for group in range(level_groups):
        level_row = group * lay.prow + place_ref[0]
        lines = packed[lay.lanes(group), :]
        extra = extra + keep_columns(lay, place_ref, seg_one, seg_two, parent, level_row, lines)
    left = halves(jnp.concatenate([solved, (extra * weight).T], axis=1))
    packed_diagonal(lay, place_ref, seg_two, left, panel_ref, out_ref, groups, paired)


def update_kernel(lay, groups, place_ref, seg_one, seg_two, parent, lower_ref, dinv_ref, *refs):
    pieces = refs[-1].shape[0]
    level_refs, piece_refs = refs[:2], refs[2 : 2 + pieces]
    out_ref, bundle_ref, panel_ref, panel_sem = refs[2 + pieces :]
    fills = start_fill(piece_refs, panel_ref, panel_sem)
    width = lay.width
    rows = lower_ref.shape[0]
    total = jnp.zeros(lower_ref.shape, F32)
    for copy in fills:
        copy.wait()
    for slot in range(lay.prow):
        source = gathered_source(lay, place_ref, slot)
        panel_part = panel_columns(lay, panel_ref, slice(None), source, place_ref[2], groups * width)
        value = level_slot(level_refs, slot)
        parts = [
            keep_columns(lay, place_ref, seg_one, seg_two, parent, group * lay.prow + source, value)
            for group in range(groups)
        ]
        total = total + product(halves(panel_part), halves(jnp.concatenate(parts, axis=0)))
    updated = lower_ref[...] - total
    out_ref[...] = updated
    bundle_ref[:rows, :] = updated
    bundle_ref[rows : rows + width, :] = level_slot(level_refs, 0)
    bundle_ref[rows + width :, :] = dinv_ref[...]


def finish_kernel(lay, count, place_ref, segment_ref, diag_ref, dinv_ref, *refs):
    turned_refs, out_ref = refs[:-1], refs[-1]
    prow_place, pcol_place = place_ref[0], place_ref[1]
    columns = diag_ref.shape[0] // lay.width
    groups = columns // lay.ratio
    upper = lax.div(prow_place, lay.pcol)
    for index, column in lay.blocks(columns):
        start = index * lay.width
        if turned_refs:
            part = (index // groups) ^ upper
            start = pl.multiple_of((part * groups + index % groups) * lay.width, lay.width)
        block = diag_ref[pl.ds(start, lay.width), :].T
        for row in range(count):
            value = block
            if turned_refs:
                even, odd = (ref[lay.lanes(row), :] for ref in turned_refs)
                value = block + jnp.where(upper == index // groups, even, odd)
            same = (
                segment_ref[row * lay.prow + prow_place]
                == segment_ref[lay.column_id(column, pcol_place)]
            )
            value = jnp.where(same, lay.read(dinv_ref, row, column, columns) + value, 0.0)
            out_ref[pl.ds(row * lay.width * columns + column, lay.width, stride=columns), :] = value


def shift_rows(piece, pairs):
    return lax.ppermute(
        piece, "prow", [(2 * source + core, 2 * target + core) for source, target in pairs for core in range(2)]
    )


def rotations(piece, prow_total):
    chips = prow_total // 2
    return [
        shift_rows(piece, [(chip, (chip + steps) % chips) for chip in range(chips)])
        for steps in range(1, chips)
    ]


def swap_cores(piece, prow_total):
    return lax.ppermute(piece, "prow", [(place, place ^ 1) for place in range(prow_total)])


PAIR_FLOWS = (((1, 0), (3, 1), (0, 2), (2, 3)), ((2, 1), (0, 3)))


def neighbour(piece, flip, pcol_total):
    return lax.ppermute(piece, "pcol", [(place, place ^ flip) for place in range(pcol_total)])


def tied(*values):
    return lax.optimization_barrier(values)


def on_device(
    root_inverse,
    lower_one,
    lower_two,
    dinv_one,
    dinv_two,
    seg_one,
    seg_two,
    parent_two,
    pattern_one,
    pattern_two,
):
    width = root_inverse.shape[2]
    prow_total = lax.axis_size("prow")
    pcol_total = lax.axis_size("pcol")
    prow_place = lax.axis_index("prow").astype(jnp.int32)
    pcol_place = lax.axis_index("pcol").astype(jnp.int32)
    lay = Layout(prow_total, pcol_total, width)
    root_count, root_columns = root_inverse.shape[0], root_inverse.shape[3]
    level_count, one_columns = dinv_one.shape[0], dinv_one.shape[3]
    second_count, two_columns = dinv_two.shape[0], dinv_two.shape[3]
    root_total = pattern_one.shape[1]
    groups_one, groups_two = one_columns // lay.ratio, two_columns // lay.ratio
    counts = (root_count, level_count, one_columns, two_columns, root_total)
    rows = root_count * width
    paired = prow_total == 8 and pcol_total == 4
    flip = pcol_place if paired else jnp.zeros_like(pcol_place)
    place = jnp.stack([prow_place, pcol_place, flip])

    def lines(argument):
        return argument.reshape(-1, width)

    first, level = vmem_call(
        functools.partial(first_kernel, lay, counts),
        (out_shape(rows, one_columns * width), out_shape(width, two_columns * width)),
        [place, seg_one, seg_two, parent_two, pattern_one, pattern_two],
        [lines(lower_one), lines(lower_two)],
    )
    root = vmem_call(
        functools.partial(root_kernel, lay, root_count, root_columns),
        out_shape(rows, root_columns * width),
        [],
        [lines(root_inverse)],
        after=[first],
    )

    root_panel = lax.all_gather(root, "pcol", axis=0, tiled=False)

    def start_panel(piece):
        if paired:
            return [neighbour(piece, 1, pcol_total), neighbour(piece, 2, pcol_total)]
        gathered = lax.all_gather(piece, "pcol", axis=0, tiled=False)
        return [gathered[source] for source in range(pcol_total)]

    def end_panel(piece, started):
        if not paired:
            return started
        beside_x, beside_y = started
        middle = piece.shape[0] // 2
        return [
            piece,
            beside_x,
            beside_y,
            neighbour(beside_y[:middle], 1, pcol_total),
            neighbour(beside_x[middle:], 2, pcol_total),
        ]

    def start_slots(piece):
        if paired:
            return [piece] + [shift_rows(piece, flow) for flow in PAIR_FLOWS]
        return [piece] + rotations(piece, prow_total)

    def both_cores(pieces):
        return pieces + [swap_cores(part, prow_total) for part in pieces]

    source_of = paired_source if paired else gathered_source
    weights = [0.5, 1.0, 1.0] * 2 if paired else [1.0] * prow_total

    first_started = start_panel(first)
    level_pieces = rotations(level, prow_total)
    first_later, level_pieces = tied(first, level_pieces)
    first_slots = start_slots(first_later)
    second_root, dinv_packed, level_own = vmem_call(
        functools.partial(second_kernel, lay, counts),
        (
            out_shape(rows, two_columns * width),
            out_shape(width, level_count * lay.ratio * width),
            out_shape(prow_total // 2, width, two_columns * width),
        ),
        [place, seg_two, parent_two, pattern_one, pattern_two],
        [lines(lower_two), lines(dinv_one), level, *level_pieces],
    )
    level_slots = [level_own, swap_cores(level_own, prow_total)]
    first_pieces = end_panel(first, first_started)
    first_pieces, level_slots, first_slots[:-1] = tied(first_pieces, level_slots, first_slots[:-1])
    first_slots = both_cores(first_slots)

    size = rows * one_columns * width
    bundle_rows = rows + 2 * width
    pieces = len(first_pieces)
    second, bundle = vmem_call(
        functools.partial(update_kernel, lay, groups_one),
        (out_shape(rows, two_columns * width), out_shape(bundle_rows, two_columns * width)),
        [place, seg_one, seg_two, parent_two],
        [second_root, dinv_packed, *level_slots],
        first_pieces,
        panel_scratch(pieces, pcol_total, rows, one_columns * width),
        flops=6 * size * seg_one.shape[0] * width,
    )
    second_slots = start_slots(second)
    bundle, first_slots = tied(bundle, first_slots)
    bundle_started = start_panel(bundle)
    packed_one = vmem_call(
        functools.partial(level_one_kernel, lay, weights, source_of, groups_one, pieces),
        out_shape(prow_total, one_columns * width, width),
        [place, seg_one],
        [],
        [root_panel, *first_pieces, *first_slots],
        panel_scratch(pieces, pcol_total, rows, one_columns * width)
        + solve_scratch(len(weights), rows, rows, one_columns * width),
        flops=6 * size * (root_total + seg_one.shape[0]) * width,
        after=[second],
    )
    packed_one, second_slots, bundle_started = tied(packed_one, second_slots, bundle_started)
    second_slots = both_cores(second_slots)
    diag_one = lax.psum_scatter(packed_one, "prow", scatter_dimension=0, tiled=False)
    bundle_pieces = end_panel(bundle, bundle_started)
    solved_two = vmem_call(
        functools.partial(solve_two_kernel, lay, weights, source_of),
        out_shape(two_columns * width, rows),
        [place],
        [],
        [root_panel, *second_slots],
        solve_scratch(len(weights), rows, rows, two_columns * width),
        flops=6 * size * root_total * width,
    )
    packed_two = vmem_call(
        functools.partial(level_two_kernel, lay, paired, weights[0], groups_two, level_count),
        out_shape(prow_total, two_columns * width, width),
        [place, seg_one, seg_two, parent_two],
        [solved_two, *level_slots],
        bundle_pieces,
        panel_scratch(pieces, pcol_total, bundle_rows, two_columns * width),
        flops=6 * size * seg_two.shape[0] * width,
    )

    diag_two = lax.psum_scatter(packed_two, "prow", scatter_dimension=0, tiled=False)

    def partners(diag, groups):
        turned = []
        for turn in range(lay.ratio):
            pairs = []
            for row in range(prow_total):
                part = (row // pcol_total) ^ turn
                for column in range(pcol_total):
                    target = (column + pcol_total * part) * pcol_total + row % pcol_total
                    pairs.append((row * pcol_total + column, target))
            sent = diag[turn * groups * width : (turn + 1) * groups * width]
            turned.append(lax.ppermute(sent, BOTH, pairs))
        return turned

    def finish(dinv, diag, segments, groups):
        count, columns = dinv.shape[0], dinv.shape[3]
        result = vmem_call(
            functools.partial(finish_kernel, lay, count),
            out_shape(count * width * columns, width),
            [place, segments],
            [diag, lines(dinv)] + (partners(diag, groups) if paired else []),
        )
        return result.reshape(dinv.shape)

    return (
        finish(dinv_one, diag_one, seg_one, groups_one),
        finish(dinv_two, diag_two, seg_two, groups_two),
    )


def solution(mesh):
    cyclic = P(None, "prow", None, None, "pcol", None)
    return jax.shard_map(
        on_device,
        mesh=mesh,
        in_specs=(cyclic,) * 5 + (P(),) * 5,
        out_specs=(cyclic, cyclic),
        check_vma=False,
    )
```
